32 devices in a mesh: member: 8 (over y, x, core), dp: 4 (over z).
Axes of the slice: x: 2, y: 2, z: 4, core: 2. Of those that a mesh axis runs over, the one named last changes fastest.
Arguments:
- teacher_tokens: bfloat16 [2752, 1536], P('dp'), may hold values from -100 to 100
- teacher_qkv: bfloat16 [8, 1536, 4608], P('member', None, 'dp'), may hold values from -0.15625 to 0.15625
- student_tokens: bfloat16 [2752, 1024], P('dp'), may hold values from -6 to 6
- student_gain: float32 [1024], replicated, may hold values from 0.1 to 1.9
- w_up: bfloat16 [1024, 4096], P(None, 'member'), may hold values from -0.1875 to 0.1875
- w_down: bfloat16 [1024, 4096], P(None, 'member'), may hold values from -0.09375 to 0.09375
- w_head: bfloat16 [1024, 1536], P(None, 'member'), may hold values from -0.1875 to 0.1875
Outputs:
- grad_up: float32 [1024, 4096], P('dp', 'member')
- grad_down: float32 [1024, 4096], P('dp', 'member')
- grad_head: float32 [1024, 1536], P('dp', 'member')
The draws below stay inside these ranges and needn't reach their ends.
All inputs are finite; a program needn't handle non-finite values.
Results may differ from the reference program's by a relative error of at most 0.0055.
Values may be sent and summed in bfloat16 or wider, within the bound.
A program may use at most 320 MiB of HBM per device.

```python
import math
from functools import partial
import jax
import jax.numpy as jnp
from jax import lax

DT = 1536
HEAD = 64
DS = 1024
FF = 4096
VALID = 1370
IMAGES = 2
TOKENS = 2752
MEMBERS = 8


def draw_teacher_tokens(key, part):
    key_base = jax.random.fold_in(key, 0)
    values = 1.6 * jnp.clip(jax.random.normal(key_base, (TOKENS, DT), jnp.float32), -6.0, 6.0)
    return values.astype(jnp.bfloat16)


def level_of(own_key, shape, cuts, low, largest):
    gain = 1.0
    for axis_at, blocks in cuts:
        heights = jax.random.uniform(jax.random.fold_in(jax.random.fold_in(own_key, 6), axis_at), (blocks,), jnp.float32, low / len(cuts), largest / len(cuts))
        gain = gain * jnp.repeat(jnp.exp(heights), shape[axis_at] // blocks).reshape((-1,) + (1,) * (len(shape) - 1 - axis_at))
    return gain


def scatter_about(key, shape, width, reach, cuts=(), kind=jnp.bfloat16):
    level = level_of(key, shape, cuts, -0.22, 0.18) if cuts else 1.0
    drawn = jax.random.normal(key, shape, jnp.float32) * width * level
    return jnp.minimum(jnp.maximum(drawn, -reach), reach).astype(kind)


def setup_inputs(seed: int = 0) -> dict:
    arg_keys = jax.random.split(jax.random.key(seed), 8)
    teacher_tokens = draw_teacher_tokens(jax.random.fold_in(arg_keys[7], 71), 0)
    teacher_qkv = scatter_about(arg_keys[1], (MEMBERS, DT, 3 * DT), DT ** -0.5, 0.15625, ((0, 8), (2, 4)))
    student_tokens = scatter_about(arg_keys[2], (TOKENS, DS), 1.0, 6.0, ((0, 4),))
    student_gain = jnp.clip(1.0 + 0.18 * jax.random.normal(arg_keys[3], (DS,), jnp.float32), 0.1, 1.9)
    w_up = scatter_about(arg_keys[4], (DS, FF), DS ** -0.5, 0.1875, ((1, 8),))
    w_down = scatter_about(arg_keys[5], (DS, FF), FF ** -0.5, 0.09375, ((1, 8),))
    w_head = scatter_about(arg_keys[6], (DS, DT), DS ** -0.5, 0.1875, ((1, 8),))
    return dict(teacher_tokens=teacher_tokens, teacher_qkv=teacher_qkv, student_tokens=student_tokens, student_gain=student_gain, w_up=w_up, w_down=w_down, w_head=w_head)


def reference(teacher_tokens, teacher_qkv, student_tokens, student_gain, w_up, w_down, w_head):
    head_count = DT // HEAD
    slots = jnp.arange(TOKENS, dtype=jnp.int32)
    image_of = slots % IMAGES
    real_slot = slots // IMAGES < VALID
    allowed = (image_of[:, None] == image_of[None, :]) & real_slot[None, :]

    def split_heads(block):
        return block.reshape(TOKENS, head_count, HEAD).transpose(1, 0, 2)

    def one_head(operands):
        query_head, key_head, value_head = operands
        scores = jnp.dot(query_head, key_head.T, preferred_element_type=jnp.float32) * 0.125
        scores = jnp.where(allowed, scores, -1e+30)
        top_score = lax.optimization_barrier(jnp.max(scores, axis=-1, keepdims=True))
        expsc = jnp.where(allowed, jnp.exp(scores - top_score), 0.0)
        denom_sum = lax.optimization_barrier(jnp.sum(expsc, axis=-1, keepdims=True))
        return jnp.dot(expsc.astype(jnp.bfloat16), value_head, preferred_element_type=jnp.float32) / denom_sum

    def member_context(running, weight):
        projected = jnp.dot(teacher_tokens, weight, preferred_element_type=jnp.float32).astype(jnp.bfloat16)
        queries = split_heads(projected[:, :DT])
        keys_all = split_heads(projected[:, DT:2 * DT])
        values_all = split_heads(projected[:, 2 * DT:])
        context = lax.map(one_head, (queries, keys_all, values_all))
        return (running + context.transpose(1, 0, 2).reshape(TOKENS, DT), None)
    summed, _ = lax.scan(member_context, jnp.zeros((TOKENS, DT), jnp.float32), teacher_qkv)
    row_mean = lax.optimization_barrier(jnp.mean(summed, axis=-1, keepdims=True))
    mean_square = lax.optimization_barrier(jnp.mean(summed * summed, axis=-1, keepdims=True))
    target = (summed - row_mean) * lax.rsqrt(mean_square - row_mean * row_mean + 1e-06)
    inputs = student_tokens.astype(jnp.float32)
    in_mean = lax.optimization_barrier(jnp.mean(inputs, axis=-1, keepdims=True))
    in_var = lax.optimization_barrier(jnp.mean((inputs - in_mean) ** 2, axis=-1, keepdims=True))
    normed = ((inputs - in_mean) * lax.rsqrt(in_var + 1e-06) * student_gain).astype(jnp.bfloat16)
    pre = jnp.dot(normed, w_up, preferred_element_type=jnp.float32)
    gelu_tanh = partial(jax.nn.gelu, approximate=True)
    hidden = gelu_tanh(pre).astype(jnp.bfloat16)
    branch = lax.dot_general(hidden, w_down, (((1,), (1,)), ((), ())), preferred_element_type=jnp.float32)
    student_out = (inputs + branch).astype(jnp.bfloat16)
    pred = jnp.dot(student_out, w_head, preferred_element_type=jnp.float32)
    pred_grad = jnp.where(real_slot[:, None], (pred - target) / math.sqrt(IMAGES * VALID), 0.0).astype(jnp.bfloat16)
    grad_head = lax.dot_general(student_out, pred_grad, (((0,), (0,)), ((), ())), preferred_element_type=jnp.float32)
    out_grad = lax.dot_general(pred_grad, w_head, (((1,), (1,)), ((), ())), preferred_element_type=jnp.float32).astype(jnp.bfloat16)
    grad_down = lax.dot_general(out_grad, hidden, (((0,), (0,)), ((), ())), preferred_element_type=jnp.float32)
    hidden_grad = jnp.dot(out_grad, w_down, preferred_element_type=jnp.float32)
    _, pullback = jax.vjp(gelu_tanh, pre)
    pre_grad = pullback(hidden_grad)[0].astype(jnp.bfloat16)
    grad_up = lax.dot_general(normed, pre_grad, (((0,), (0,)), ((), ())), preferred_element_type=jnp.float32)
    return (grad_up, grad_down, grad_head)
```

```python
from functools import partial
import math

import jax
import jax.numpy as jnp
from jax import lax
from jax.experimental import pallas as pl
from jax.experimental.pallas import tpu as pltpu
from jax.sharding import PartitionSpec as P

VALID = 1370
IMAGES = 2
HEAD = 64
PAIR = 2 * HEAD
ROWS = 16


def attention_kernel(tile, q_ref, k_ref, v_ref, bias_ref, out_ref):
    rows = q_ref.shape[1]
    lane = lax.broadcasted_iota(jnp.int32, (rows, PAIR), 1)
    keys, values = k_ref[0], v_ref[0]
    bias = bias_ref[...]
    sides = []
    for head in range(2):
        own = (lane < HEAD) if head == 0 else (lane >= HEAD)
        sides.append((jnp.where(own, keys, bias), jnp.where(own, values, jnp.ones_like(values))))
    tile_lane = lax.broadcasted_iota(jnp.int32, (tile, PAIR), 1)
    for at in range(rows // tile):
        queries = q_ref[0, at * tile : (at + 1) * tile, :] * jnp.asarray(0.125, jnp.bfloat16)
        parts = []
        for head in range(2):
            own = (tile_lane < HEAD) if head == 0 else (tile_lane >= HEAD)
            mark = jnp.where(tile_lane == (1 - head) * HEAD, 1.0, 0.0).astype(jnp.bfloat16)
            scores = lax.dot_general(
                jnp.where(own, queries, mark), sides[head][0], (((1,), (1,)), ((), ())),
                preferred_element_type=jnp.float32,
            )
            top = jnp.max(scores, axis=-1, keepdims=True)
            probs = jnp.exp(scores - top).astype(jnp.bfloat16)
            mixed = jnp.dot(probs, sides[head][1], preferred_element_type=jnp.float32)
            parts.append(mixed / pltpu.roll(mixed, HEAD, 1))
        joined = jnp.where(tile_lane < HEAD, parts[0], parts[1])
        out_ref[0, at * tile : (at + 1) * tile, :] = joined.astype(out_ref.dtype)


def attention(projected, bias):
    images, rows, width = projected.shape
    pairs = width // 3 // PAIR
    tile = rows // 4 if rows % (4 * ROWS) == 0 else rows
    block = lambda first: pl.BlockSpec((1, rows, PAIR), lambda i, p: (i, 0, first + p))
    return pl.pallas_call(
        partial(attention_kernel, tile),
        grid=(images, pairs),
        in_specs=[block(0), block(pairs), block(2 * pairs), pl.BlockSpec((rows, PAIR), lambda i, p: (0, 0))],
        out_specs=pl.BlockSpec((1, rows, PAIR), lambda i, p: (i, 0, p)),
        out_shape=jax.ShapeDtypeStruct((images, rows, width // 3), jnp.bfloat16),
        compiler_params=pltpu.CompilerParams(vmem_limit_bytes=48 * 1024 * 1024),
        cost_estimate=pl.CostEstimate(
            flops=images * pairs * 2 * rows * rows * PAIR * 4,
            bytes_accessed=images * rows * width * 3,
            transcendentals=images * pairs * 2 * rows * rows,
        ),
        name="attention",
    )(projected, projected, projected, bias)


def by_image(tokens, slot_rows):
    rows, width = tokens.shape
    split = tokens.reshape(rows // IMAGES, IMAGES, width).transpose(1, 0, 2)
    return jnp.pad(split, ((0, 0), (0, slot_rows - rows // IMAGES), (0, 0)))


def gather_teacher(tokens, weights, dp, member):
    images, rows, width = tokens.shape
    share = width * images // member
    me = lax.axis_index("member")
    block = lax.dynamic_slice(tokens, (me % images, 0, (me // images) * share), (1, rows, share))[0]
    column = lax.all_gather(block, "dp", axis=0, tiled=True)
    every = lax.all_gather(column, "member", axis=0, tiled=False)
    every = every.reshape(member // images, images, dp * rows, share).transpose(1, 2, 0, 3)
    every = every.reshape(images, dp * rows, width)
    piece = weights.shape[1] // 3
    came = []
    for j in range(3):
        pairs = [(s, (3 * s + j) % dp) for s in range(dp)]
        came.append(lax.ppermute(weights[:, j * piece : (j + 1) * piece], "dp", pairs))
    came = jnp.stack(came)
    at = lax.axis_index("dp")
    table = [[0] * 3 for _ in range(dp)]
    for s in range(dp):
        for j in range(3):
            table[(3 * s + j) % dp][(3 * s + j) // dp] = j
    order = jnp.asarray(table, jnp.int32)[at]
    own = [lax.dynamic_index_in_dim(came, order[c], 0, keepdims=False) for c in range(3)]
    return every, jnp.concatenate(own, axis=1)


def split_body(dp, member, teacher_tokens, teacher_qkv, student_tokens, student_gain, w_up, w_down, w_head):
    part_rows = teacher_tokens.shape[0] // IMAGES
    slot_rows = -(-part_rows // ROWS) * ROWS
    own_rows = IMAGES * slot_rows // member
    quarter = slot_rows // own_rows
    dp_at, member_at = lax.axis_index("dp"), lax.axis_index("member")

    tokens, weights = gather_teacher(by_image(teacher_tokens, slot_rows), teacher_qkv[0], dp, member)

    student = by_image(student_tokens, slot_rows).reshape(IMAGES * slot_rows, -1)
    inputs = student.astype(jnp.float32)
    in_mean = jnp.mean(inputs, axis=-1, keepdims=True)
    in_var = jnp.mean((inputs - in_mean) ** 2, axis=-1, keepdims=True)
    normed = ((inputs - in_mean) * lax.rsqrt(in_var + 1e-06) * student_gain).astype(jnp.bfloat16)
    pre = jnp.dot(normed, w_up, preferred_element_type=jnp.float32)
    gelu_tanh = partial(jax.nn.gelu, approximate=True)
    hidden = gelu_tanh(pre).astype(jnp.bfloat16)
    branch_part = lax.dot_general(
        hidden, w_down, (((1,), (1,)), ((), ())), preferred_element_type=jnp.float32
    )
    branch = lax.psum_scatter(branch_part, "member", scatter_dimension=0, tiled=True)
    own_inputs = lax.dynamic_slice_in_dim(student, member_at * own_rows, own_rows, 0).astype(jnp.float32)
    own_out = (own_inputs + branch).astype(jnp.bfloat16)
    student_out = lax.all_gather(own_out, "member", axis=0, tiled=True)
    head_all = lax.all_gather(w_head, "member", axis=1, tiled=True)

    images, rows, width = tokens.shape
    projected = jnp.dot(
        tokens.reshape(images * rows, width), weights, preferred_element_type=jnp.float32
    ).astype(jnp.bfloat16).reshape(images, rows, -1)
    key_row = jnp.arange(rows, dtype=jnp.int32)
    in_part = key_row % slot_rows
    real_key = (in_part < part_rows) & (key_row // slot_rows * part_rows + in_part < VALID)
    bias = jnp.broadcast_to(jnp.where(real_key, 0.0, -1e30).astype(jnp.bfloat16)[:, None], (rows, PAIR))
    context = attention(projected, bias)
    share = context.shape[-1]
    context = context.reshape(images, dp, quarter, own_rows, share).transpose(0, 2, 1, 3, 4)
    context = context.reshape(member, dp * own_rows, share)
    summed = lax.psum_scatter(context, "member", scatter_dimension=0, tiled=False)
    summed = lax.all_to_all(summed.reshape(dp, own_rows, share), "dp", 0, 0, tiled=False)
    summed = summed.transpose(1, 0, 2).reshape(own_rows, width).astype(jnp.float32)
    row_mean = jnp.mean(summed, axis=-1, keepdims=True)
    mean_square = jnp.mean(summed * summed, axis=-1, keepdims=True)
    target = (summed - row_mean) * lax.rsqrt(mean_square - row_mean * row_mean + 1e-06)

    own_row = (member_at % quarter) * own_rows + jnp.arange(own_rows, dtype=jnp.int32)
    real = (own_row < part_rows) & (dp_at * part_rows + own_row < VALID)
    pred = jnp.dot(own_out, head_all, preferred_element_type=jnp.float32)
    own_grad = jnp.where(real[:, None], (pred - target) / math.sqrt(IMAGES * VALID), 0.0).astype(jnp.bfloat16)
    pred_grad = lax.all_gather(own_grad, "member", axis=0, tiled=True)
    head_width = w_head.shape[1]
    own_columns = lax.dynamic_slice_in_dim(pred_grad, member_at * head_width, head_width, 1)
    out_grad = lax.dot_general(
        pred_grad, head_all, (((1,), (1,)), ((), ())), preferred_element_type=jnp.float32
    ).astype(jnp.bfloat16)
    grad_down = lax.dot_general(
        out_grad, hidden, (((0,), (0,)), ((), ())), preferred_element_type=jnp.float32
    )
    hidden_grad = jnp.dot(out_grad, w_down, preferred_element_type=jnp.float32)
    _, pullback = jax.vjp(gelu_tanh, pre)
    pre_grad = pullback(hidden_grad)[0].astype(jnp.bfloat16)
    grad_up = lax.dot_general(
        normed, pre_grad, (((0,), (0,)), ((), ())), preferred_element_type=jnp.float32
    )
    grad_head = lax.dot_general(
        student_out, own_columns, (((0,), (0,)), ((), ())), preferred_element_type=jnp.float32
    )
    return tuple(
        lax.psum_scatter(g, "dp", scatter_dimension=0, tiled=True) for g in (grad_up, grad_down, grad_head)
    )


def body(teacher_tokens, teacher_qkv, student_tokens, student_gain, w_up, w_down, w_head):
    tok_rows = teacher_tokens.shape[0]
    feat_width = teacher_tokens.shape[1]
    head_count = feat_width // 64
    own_columns = teacher_qkv[0]
    query_slots = lax.axis_index("dp") * tok_rows + jnp.arange(tok_rows, dtype=jnp.int32)
    query_image = query_slots % IMAGES
    real_query = query_slots // IMAGES < VALID
    projected = jnp.dot(
        teacher_tokens,
        lax.all_gather(own_columns, "dp", axis=1, tiled=True),
        preferred_element_type=jnp.float32,
    ).astype(jnp.bfloat16)
    queries = projected[:, :feat_width].reshape(tok_rows, head_count, 64)
    keys_local = projected[:, feat_width : 2 * feat_width]
    values_local = projected[:, 2 * feat_width :]
    row_max = jnp.full((head_count, tok_rows), -1e30, jnp.float32)
    weighted = jnp.zeros((tok_rows, head_count, 64), jnp.float32)
    key_heads = lax.all_gather(keys_local, "dp", axis=0, tiled=True).reshape(-1, head_count, 64)
    value_heads = lax.all_gather(values_local, "dp", axis=0, tiled=True).reshape(-1, head_count, 64)
    key_slots = jnp.arange(key_heads.shape[0], dtype=jnp.int32)
    allowed = (query_image[:, None] == (key_slots % IMAGES)[None, :]) & (
        key_slots // IMAGES < VALID
    )[None, :]
    scores = (
        jnp.einsum("qhd,khd->hqk", queries, key_heads, preferred_element_type=jnp.float32) * 0.125
    )
    scores = jnp.where(allowed[None], scores, -1e30)
    new_max = jnp.maximum(row_max, jnp.max(scores, axis=-1))
    factor = jnp.exp(row_max - new_max)
    expsc = jnp.where(allowed[None], jnp.exp(scores - new_max[:, :, None]), 0.0)
    denom_sum = jnp.sum(expsc, axis=-1)
    update = jnp.einsum(
        "hqk,khd->qhd", expsc.astype(jnp.bfloat16), value_heads, preferred_element_type=jnp.float32
    )
    weighted = weighted * factor.T[:, :, None] + update
    row_max, denom_sum, weighted = (new_max, denom_sum, weighted)
    context = (weighted / denom_sum.T[:, :, None]).reshape(tok_rows, feat_width)
    member_slot = lax.axis_index("member")
    share_width = feat_width // lax.axis_size("member")
    summed = lax.psum(context, "member")
    row_mean = jnp.mean(summed, axis=-1, keepdims=True)
    mean_square = jnp.mean(summed * summed, axis=-1, keepdims=True)
    full_target = (summed - row_mean) * lax.rsqrt(mean_square - row_mean * row_mean + 1e-06)
    target = lax.dynamic_slice_in_dim(full_target, member_slot * share_width, share_width, 1)
    inputs = student_tokens.astype(jnp.float32)
    in_mean = jnp.mean(inputs, axis=-1, keepdims=True)
    in_var = jnp.mean((inputs - in_mean) ** 2, axis=-1, keepdims=True)
    normed = ((inputs - in_mean) * lax.rsqrt(in_var + 1e-06) * student_gain).astype(jnp.bfloat16)
    pre = jnp.dot(normed, w_up, preferred_element_type=jnp.float32)
    gelu_tanh = partial(jax.nn.gelu, approximate=True)
    hidden = gelu_tanh(pre).astype(jnp.bfloat16)
    branch_part = lax.dot_general(
        hidden, w_down, (((1,), (1,)), ((), ())), preferred_element_type=jnp.float32
    )
    student_out = (inputs + lax.psum(branch_part, "member")).astype(jnp.bfloat16)
    pred = jnp.dot(student_out, w_head, preferred_element_type=jnp.float32)
    pred_grad = jnp.where(
        real_query[:, None], (pred - target) / math.sqrt(IMAGES * VALID), 0.0
    ).astype(jnp.bfloat16)
    grad_head = lax.dot_general(
        student_out, pred_grad, (((0,), (0,)), ((), ())), preferred_element_type=jnp.float32
    )
    out_part = lax.dot_general(
        pred_grad, w_head, (((1,), (1,)), ((), ())), preferred_element_type=jnp.float32
    )
    out_grad = lax.psum(out_part, "member").astype(jnp.bfloat16)
    grad_down = lax.dot_general(
        out_grad, hidden, (((0,), (0,)), ((), ())), preferred_element_type=jnp.float32
    )
    hidden_grad = jnp.dot(out_grad, w_down, preferred_element_type=jnp.float32)
    _, pullback = jax.vjp(gelu_tanh, pre)
    pre_grad = pullback(hidden_grad)[0].astype(jnp.bfloat16)
    grad_up = lax.dot_general(
        normed, pre_grad, (((0,), (0,)), ((), ())), preferred_element_type=jnp.float32
    )
    grad_up, grad_down, grad_head = (
        lax.psum_scatter(grad_up, "dp", scatter_dimension=0, tiled=True),
        lax.psum_scatter(grad_down, "dp", scatter_dimension=0, tiled=True),
        lax.psum_scatter(grad_head, "dp", scatter_dimension=0, tiled=True),
    )
    return (grad_up, grad_down, grad_head)


def can_split(dp, member, tokens, feat):
    slot_rows = -(-(tokens // dp // IMAGES) // ROWS) * ROWS
    return (
        math.gcd(3, dp) == 1
        and feat % (dp * PAIR) == 0
        and member % IMAGES == 0
        and (feat * IMAGES) % (member * PAIR) == 0
        and slot_rows * IMAGES % (member * 8) == 0
    )


def solution(mesh):
    in_specs = (
        P("dp", None),
        P("member", None, "dp"),
        P("dp", None),
        P(),
        P(None, "member"),
        P(None, "member"),
        P(None, "member"),
    )
    out_specs = (P("dp", "member"), P("dp", "member"), P("dp", "member"))

    def run(teacher_tokens, *rest):
        dp, member = mesh.shape["dp"], mesh.shape["member"]
        part = body
        if can_split(dp, member, *teacher_tokens.shape):
            part = partial(split_body, dp, member)
        call = jax.shard_map(part, mesh=mesh, in_specs=in_specs, out_specs=out_specs, check_vma=False)
        return call(teacher_tokens, *rest)

    return run
```

```python
from functools import partial
import math

import jax
import jax.numpy as jnp
from jax import lax
from jax.experimental import pallas as pl
from jax.experimental.pallas import tpu as pltpu
from jax.sharding import PartitionSpec as P

VALID = 1370
IMAGES = 2
HEAD = 64
PAIR = 2 * HEAD
ROWS = 16


def attention_kernel(tile, q_ref, k_ref, v_ref, bias_ref, out_ref):
    rows = q_ref.shape[1]
    lane = lax.broadcasted_iota(jnp.int32, (rows, PAIR), 1)
    keys, values = k_ref[0], v_ref[0]
    bias = bias_ref[...]
    sides = []
    for head in range(2):
        own = (lane < HEAD) if head == 0 else (lane >= HEAD)
        sides.append((jnp.where(own, keys, bias), jnp.where(own, values, jnp.ones_like(values))))
    tile_lane = lax.broadcasted_iota(jnp.int32, (tile, PAIR), 1)
    for at in range(rows // tile):
        queries = q_ref[0, at * tile : (at + 1) * tile, :] * jnp.asarray(0.125, jnp.bfloat16)
        parts = []
        for head in range(2):
            own = (tile_lane < HEAD) if head == 0 else (tile_lane >= HEAD)
            mark = jnp.where(tile_lane == (1 - head) * HEAD, 1.0, 0.0).astype(jnp.bfloat16)
            scores = lax.dot_general(
                jnp.where(own, queries, mark), sides[head][0], (((1,), (1,)), ((), ())),
                preferred_element_type=jnp.float32,
            )
            top = jnp.max(scores, axis=-1, keepdims=True)
            probs = jnp.exp(scores - top).astype(jnp.bfloat16)
            mixed = jnp.dot(probs, sides[head][1], preferred_element_type=jnp.float32)
            parts.append(mixed / pltpu.roll(mixed, HEAD, 1))
        joined = jnp.where(tile_lane < HEAD, parts[0], parts[1])
        out_ref[0, at * tile : (at + 1) * tile, :] = joined.astype(out_ref.dtype)


def attention(projected, bias):
    images, rows, width = projected.shape
    pairs = width // 3 // PAIR
    tile = rows // 4 if rows % (4 * ROWS) == 0 else rows
    block = lambda first: pl.BlockSpec((1, rows, PAIR), lambda i, p: (i, 0, first + p))
    return pl.pallas_call(
        partial(attention_kernel, tile),
        grid=(images, pairs),
        in_specs=[block(0), block(pairs), block(2 * pairs), pl.BlockSpec((rows, PAIR), lambda i, p: (0, 0))],
        out_specs=pl.BlockSpec((1, rows, PAIR), lambda i, p: (i, 0, p)),
        out_shape=jax.ShapeDtypeStruct((images, rows, width // 3), jnp.bfloat16),
        compiler_params=pltpu.CompilerParams(vmem_limit_bytes=48 * 1024 * 1024),
        cost_estimate=pl.CostEstimate(
            flops=images * pairs * 2 * rows * rows * PAIR * 4,
            bytes_accessed=images * rows * width * 3,
            transcendentals=images * pairs * 2 * rows * rows,
        ),
        name="attention",
    )(projected, projected, projected, bias)


def by_image(tokens, slot_rows):
    rows, width = tokens.shape
    split = tokens.reshape(rows // IMAGES, IMAGES, width).transpose(1, 0, 2)
    return jnp.pad(split, ((0, 0), (0, slot_rows - rows // IMAGES), (0, 0)))


def gather_kernel(dp, src, wts, tok, own, z_send, z_recv, p_send, p_recv, f_send, f_recv, w_send, w_recv, local):
    rows, width = src.shape[1], src.shape[2]
    depth, piece = wts.shape[0], wts.shape[1] // 3
    m, z = lax.axis_index("member"), lax.axis_index("dp")
    core, x, y = m % 2, (m // 2) % 2, m // 4
    chips = 4
    share = width // chips
    other_core = m + 1 - 2 * core
    to_x, to_y = 2 - 4 * x, 4 - 8 * y
    peers = [m + to_x, m + to_y, m + to_x + to_y, other_core]

    barrier = pltpu.get_barrier_semaphore()
    for k in range(1, dp):
        pl.semaphore_signal(
            barrier, inc=1, device_id={"member": m, "dp": (z + k) % dp}, device_id_type=pl.DeviceIdType.MESH
        )
    for peer in peers:
        pl.semaphore_signal(
            barrier, inc=1, device_id={"member": peer, "dp": z}, device_id_type=pl.DeviceIdType.MESH
        )
    pl.semaphore_wait(barrier, dp - 1 + len(peers))

    def columns(chip):
        return pl.ds(pl.multiple_of(chip * share, PAIR), share)

    def region(image, part, chip):
        return tok.at[image, pl.ds(pl.multiple_of(part * rows, ROWS), rows), columns(chip)]

    def send(source, target, sems, member, part):
        return pltpu.make_async_remote_copy(
            src_ref=source, dst_ref=target, send_sem=sems[0], recv_sem=sems[1],
            device_id={"member": member, "dp": part}, device_id_type=pl.DeviceIdType.MESH,
        )

    chip = m // 2
    first = []
    for k in range(1, dp):
        copy = send(
            src.at[core, :, columns(chip)], region(core, z, chip),
            (z_send.at[k - 1], z_recv.at[k - 1]), m, (z + k) % dp,
        )
        copy.start()
        first.append(copy)
    stay = pltpu.make_async_copy(src, tok.at[:, pl.ds(pl.multiple_of(z * rows, ROWS), rows), :], local.at[3])
    stay.start()

    def weight_copy(j):
        dest, slot = (3 * z + j) % dp, (3 * z + j) // dp
        source = wts.at[:, pl.ds(j * piece, piece)]
        target = own.at[:, pl.ds(pl.multiple_of(slot * piece, PAIR), piece)]
        return dest, source, target, slot

    for j in range(3):
        dest, source, target, slot = weight_copy(j)

        @pl.when(dest == z)
        def _():
            pltpu.make_async_copy(source, target, local.at[j]).start()

        @pl.when(dest != z)
        def _():
            send(source, target, (w_send.at[j], w_recv.at[slot]), m, dest).start()

    passed = []
    for k in range(1, dp):
        part = (z + dp - k) % dp
        here = region(core, part, chip)
        first[k - 1].wait_recv()
        for p, peer in enumerate(peers):
            copy = send(here, here, (p_send.at[k - 1, p], p_recv.at[k - 1, p]), peer, z)
            copy.start()
            passed.append(copy)
    chips_of = [(m + to_x) // 2, (m + to_y) // 2, (m + to_x + to_y) // 2]
    for k in range(1, dp):
        part = (z + dp - k) % dp
        for p in range(3):
            here = region(core, part, chips_of[p])
            send(here, here, (p_send.at[k - 1, p], p_recv.at[k - 1, p]), other_core, z).wait_recv()
            copy = send(here, here, (f_send.at[k - 1, p], f_recv.at[k - 1, p]), other_core, z)
            copy.start()
            passed.append(copy)
    for k in range(1, dp):
        part = (z + dp - k) % dp
        there = region(1 - core, part, chip)
        send(there, there, (p_send.at[k - 1, 3], p_recv.at[k - 1, 3]), other_core, z).wait_recv()
        for p in range(3):
            there = region(1 - core, part, chips_of[p])
            send(there, there, (f_send.at[k - 1, p], f_recv.at[k - 1, p]), other_core, z).wait_recv()
    for copy in first + passed:
        copy.wait_send()
    for j in range(3):
        dest, source, target, slot = weight_copy(j)

        @pl.when(dest == z)
        def _():
            pltpu.make_async_copy(source, target, local.at[j]).wait()

        @pl.when(dest != z)
        def _():
            send(source, target, (w_send.at[j], w_recv.at[slot]), m, dest).wait_send()

    for slot in range(3):
        place = own.at[:, pl.ds(slot * piece, piece)]

        @pl.when((slot * dp + z) // 3 != z)
        def _():
            send(place, place, (w_send.at[0], w_recv.at[slot]), m, (z + 1) % dp).wait_recv()

    stay.wait()


def gather_teacher(tokens, weights, dp):
    images, rows, width = tokens.shape
    steps = dp - 1
    dma = pltpu.SemaphoreType.DMA
    return pl.pallas_call(
        partial(gather_kernel, dp),
        out_shape=(
            jax.ShapeDtypeStruct((images, dp * rows, width), tokens.dtype),
            jax.ShapeDtypeStruct(weights.shape, weights.dtype),
        ),
        in_specs=[pl.BlockSpec(memory_space=pl.ANY)] * 2,
        out_specs=(pl.BlockSpec(memory_space=pl.ANY),) * 2,
        scratch_shapes=[
            dma((steps,)), dma((steps,)), dma((steps, 4)), dma((steps, 4)), dma((steps, 3)), dma((steps, 3)),
            dma((3,)), dma((3,)), dma((4,)),
        ],
        compiler_params=pltpu.CompilerParams(collective_id=0, has_side_effects=True),
        cost_estimate=pl.CostEstimate(
            flops=0, bytes_accessed=64 * images * dp * rows * width, transcendentals=0
        ),
        name="gather_teacher",
    )(tokens, weights)


def split_body(dp, member, teacher_tokens, teacher_qkv, student_tokens, student_gain, w_up, w_down, w_head):
    part_rows = teacher_tokens.shape[0] // IMAGES
    slot_rows = -(-part_rows // ROWS) * ROWS
    own_rows = IMAGES * slot_rows // member
    quarter = slot_rows // own_rows
    dp_at, member_at = lax.axis_index("dp"), lax.axis_index("member")

    student = by_image(student_tokens, slot_rows).reshape(IMAGES * slot_rows, -1)
    inputs = student.astype(jnp.float32)
    in_mean = jnp.mean(inputs, axis=-1, keepdims=True)
    in_var = jnp.mean((inputs - in_mean) ** 2, axis=-1, keepdims=True)
    normed = ((inputs - in_mean) * lax.rsqrt(in_var + 1e-06) * student_gain).astype(jnp.bfloat16)
    pre = jnp.dot(normed, w_up, preferred_element_type=jnp.float32)
    gelu_tanh = partial(jax.nn.gelu, approximate=True)
    hidden = gelu_tanh(pre).astype(jnp.bfloat16)
    branch_part = lax.dot_general(
        hidden, w_down, (((1,), (1,)), ((), ())), preferred_element_type=jnp.float32
    )
    teacher_slots, branch_part = lax.optimization_barrier((by_image(teacher_tokens, slot_rows), branch_part))
    tokens, weights = gather_teacher(teacher_slots, teacher_qkv[0], dp)
    branch = lax.psum_scatter(branch_part, "member", scatter_dimension=0, tiled=True)
    own_inputs = lax.dynamic_slice_in_dim(student, member_at * own_rows, own_rows, 0).astype(jnp.float32)
    own_out = (own_inputs + branch).astype(jnp.bfloat16)
    head_all = lax.all_gather(w_head, "member", axis=1, tiled=True)

    images, rows, width = tokens.shape
    projected = jnp.dot(
        tokens.reshape(images * rows, width), weights, preferred_element_type=jnp.float32
    ).astype(jnp.bfloat16).reshape(images, rows, -1)
    key_row = jnp.arange(rows, dtype=jnp.int32)
    in_part = key_row % slot_rows
    real_key = (in_part < part_rows) & (key_row // slot_rows * part_rows + in_part < VALID)
    bias = jnp.broadcast_to(jnp.where(real_key, 0.0, -1e30).astype(jnp.bfloat16)[:, None], (rows, PAIR))
    projected, student_out_own = lax.optimization_barrier((projected, own_out))
    student_out = lax.all_gather(student_out_own, "member", axis=0, tiled=True)
    context = attention(projected, bias)
    share = context.shape[-1]
    context = context.reshape(images, dp, quarter, own_rows, share).transpose(0, 2, 1, 3, 4)
    context = context.reshape(member, dp * own_rows, share)
    summed = lax.psum_scatter(context, "member", scatter_dimension=0, tiled=False)
    summed = lax.all_to_all(summed.reshape(dp, own_rows, share), "dp", 0, 0, tiled=False)
    summed = summed.transpose(1, 0, 2).reshape(own_rows, width).astype(jnp.float32)
    row_mean = jnp.mean(summed, axis=-1, keepdims=True)
    mean_square = jnp.mean(summed * summed, axis=-1, keepdims=True)
    target = (summed - row_mean) * lax.rsqrt(mean_square - row_mean * row_mean + 1e-06)

    own_row = (member_at % quarter) * own_rows + jnp.arange(own_rows, dtype=jnp.int32)
    real = (own_row < part_rows) & (dp_at * part_rows + own_row < VALID)
    pred = jnp.dot(own_out, head_all, preferred_element_type=jnp.float32)
    own_grad = jnp.where(real[:, None], (pred - target) / math.sqrt(IMAGES * VALID), 0.0).astype(jnp.bfloat16)
    pred_grad = lax.all_gather(own_grad, "member", axis=0, tiled=True)
    head_width = w_head.shape[1]
    own_columns = lax.dynamic_slice_in_dim(pred_grad, member_at * head_width, head_width, 1)
    out_grad = lax.dot_general(
        pred_grad, head_all, (((1,), (1,)), ((), ())), preferred_element_type=jnp.float32
    ).astype(jnp.bfloat16)
    grad_down = lax.dot_general(
        out_grad, hidden, (((0,), (0,)), ((), ())), preferred_element_type=jnp.float32
    )
    hidden_grad = jnp.dot(out_grad, w_down, preferred_element_type=jnp.float32)
    _, pullback = jax.vjp(gelu_tanh, pre)
    pre_grad = pullback(hidden_grad)[0].astype(jnp.bfloat16)
    grad_up = lax.dot_general(
        normed, pre_grad, (((0,), (0,)), ((), ())), preferred_element_type=jnp.float32
    )
    grad_head = lax.dot_general(
        student_out, own_columns, (((0,), (0,)), ((), ())), preferred_element_type=jnp.float32
    )
    return tuple(
        lax.psum_scatter(g.astype(jnp.bfloat16), "dp", scatter_dimension=0, tiled=True).astype(jnp.float32)
        for g in (grad_up, grad_down, grad_head)
    )


def body(teacher_tokens, teacher_qkv, student_tokens, student_gain, w_up, w_down, w_head):
    tok_rows = teacher_tokens.shape[0]
    feat_width = teacher_tokens.shape[1]
    head_count = feat_width // 64
    own_columns = teacher_qkv[0]
    query_slots = lax.axis_index("dp") * tok_rows + jnp.arange(tok_rows, dtype=jnp.int32)
    query_image = query_slots % IMAGES
    real_query = query_slots // IMAGES < VALID
    projected = jnp.dot(
        teacher_tokens,
        lax.all_gather(own_columns, "dp", axis=1, tiled=True),
        preferred_element_type=jnp.float32,
    ).astype(jnp.bfloat16)
    queries = projected[:, :feat_width].reshape(tok_rows, head_count, 64)
    keys_local = projected[:, feat_width : 2 * feat_width]
    values_local = projected[:, 2 * feat_width :]
    row_max = jnp.full((head_count, tok_rows), -1e30, jnp.float32)
    weighted = jnp.zeros((tok_rows, head_count, 64), jnp.float32)
    key_heads = lax.all_gather(keys_local, "dp", axis=0, tiled=True).reshape(-1, head_count, 64)
    value_heads = lax.all_gather(values_local, "dp", axis=0, tiled=True).reshape(-1, head_count, 64)
    key_slots = jnp.arange(key_heads.shape[0], dtype=jnp.int32)
    allowed = (query_image[:, None] == (key_slots % IMAGES)[None, :]) & (
        key_slots // IMAGES < VALID
    )[None, :]
    scores = (
        jnp.einsum("qhd,khd->hqk", queries, key_heads, preferred_element_type=jnp.float32) * 0.125
    )
    scores = jnp.where(allowed[None], scores, -1e30)
    new_max = jnp.maximum(row_max, jnp.max(scores, axis=-1))
    factor = jnp.exp(row_max - new_max)
    expsc = jnp.where(allowed[None], jnp.exp(scores - new_max[:, :, None]), 0.0)
    denom_sum = jnp.sum(expsc, axis=-1)
    update = jnp.einsum(
        "hqk,khd->qhd", expsc.astype(jnp.bfloat16), value_heads, preferred_element_type=jnp.float32
    )
    weighted = weighted * factor.T[:, :, None] + update
    row_max, denom_sum, weighted = (new_max, denom_sum, weighted)
    context = (weighted / denom_sum.T[:, :, None]).reshape(tok_rows, feat_width)
    member_slot = lax.axis_index("member")
    share_width = feat_width // lax.axis_size("member")
    summed = lax.psum(context, "member")
    row_mean = jnp.mean(summed, axis=-1, keepdims=True)
    mean_square = jnp.mean(summed * summed, axis=-1, keepdims=True)
    full_target = (summed - row_mean) * lax.rsqrt(mean_square - row_mean * row_mean + 1e-06)
    target = lax.dynamic_slice_in_dim(full_target, member_slot * share_width, share_width, 1)
    inputs = student_tokens.astype(jnp.float32)
    in_mean = jnp.mean(inputs, axis=-1, keepdims=True)
    in_var = jnp.mean((inputs - in_mean) ** 2, axis=-1, keepdims=True)
    normed = ((inputs - in_mean) * lax.rsqrt(in_var + 1e-06) * student_gain).astype(jnp.bfloat16)
    pre = jnp.dot(normed, w_up, preferred_element_type=jnp.float32)
    gelu_tanh = partial(jax.nn.gelu, approximate=True)
    hidden = gelu_tanh(pre).astype(jnp.bfloat16)
    branch_part = lax.dot_general(
        hidden, w_down, (((1,), (1,)), ((), ())), preferred_element_type=jnp.float32
    )
    student_out = (inputs + lax.psum(branch_part, "member")).astype(jnp.bfloat16)
    pred = jnp.dot(student_out, w_head, preferred_element_type=jnp.float32)
    pred_grad = jnp.where(
        real_query[:, None], (pred - target) / math.sqrt(IMAGES * VALID), 0.0
    ).astype(jnp.bfloat16)
    grad_head = lax.dot_general(
        student_out, pred_grad, (((0,), (0,)), ((), ())), preferred_element_type=jnp.float32
    )
    out_part = lax.dot_general(
        pred_grad, w_head, (((1,), (1,)), ((), ())), preferred_element_type=jnp.float32
    )
    out_grad = lax.psum(out_part, "member").astype(jnp.bfloat16)
    grad_down = lax.dot_general(
        out_grad, hidden, (((0,), (0,)), ((), ())), preferred_element_type=jnp.float32
    )
    hidden_grad = jnp.dot(out_grad, w_down, preferred_element_type=jnp.float32)
    _, pullback = jax.vjp(gelu_tanh, pre)
    pre_grad = pullback(hidden_grad)[0].astype(jnp.bfloat16)
    grad_up = lax.dot_general(
        normed, pre_grad, (((0,), (0,)), ((), ())), preferred_element_type=jnp.float32
    )
    grad_up, grad_down, grad_head = (
        lax.psum_scatter(grad_up, "dp", scatter_dimension=0, tiled=True),
        lax.psum_scatter(grad_down, "dp", scatter_dimension=0, tiled=True),
        lax.psum_scatter(grad_head, "dp", scatter_dimension=0, tiled=True),
    )
    return (grad_up, grad_down, grad_head)


def can_split(dp, member, tokens, feat):
    slot_rows = -(-(tokens // dp // IMAGES) // ROWS) * ROWS
    return (
        math.gcd(3, dp) == 1
        and feat % (dp * PAIR) == 0
        and member == 4 * IMAGES
        and feat % (4 * PAIR) == 0
        and slot_rows * IMAGES % (member * 8) == 0
    )


def solution(mesh):
    in_specs = (
        P("dp", None),
        P("member", None, "dp"),
        P("dp", None),
        P(),
        P(None, "member"),
        P(None, "member"),
        P(None, "member"),
    )
    out_specs = (P("dp", "member"), P("dp", "member"), P("dp", "member"))

    def run(teacher_tokens, *rest):
        dp, member = mesh.shape["dp"], mesh.shape["member"]
        part = body
        if can_split(dp, member, *teacher_tokens.shape):
            part = partial(split_body, dp, member)
        call = jax.shard_map(part, mesh=mesh, in_specs=in_specs, out_specs=out_specs, check_vma=False)
        return call(teacher_tokens, *rest)

    return run
```

```python
from functools import partial
import math

import jax
import jax.numpy as jnp
from jax import lax
from jax.experimental import pallas as pl
from jax.experimental.pallas import tpu as pltpu
from jax.sharding import PartitionSpec as P

VALID = 1370
IMAGES = 2
HEAD = 64
PAIR = 2 * HEAD
ROWS = 16


def attention_kernel(tile, q_ref, k_ref, v_ref, bias_ref, out_ref):
    rows = q_ref.shape[1]
    lane = lax.broadcasted_iota(jnp.int32, (rows, PAIR), 1)
    keys, values = k_ref[0], v_ref[0]
    bias = bias_ref[...]
    sides = []
    for head in range(2):
        own = (lane < HEAD) if head == 0 else (lane >= HEAD)
        sides.append((jnp.where(own, keys, bias), jnp.where(own, values, jnp.ones_like(values))))
    tile_lane = lax.broadcasted_iota(jnp.int32, (tile, PAIR), 1)
    for at in range(rows // tile):
        queries = q_ref[0, at * tile : (at + 1) * tile, :] * jnp.asarray(0.125, jnp.bfloat16)
        parts = []
        for head in range(2):
            own = (tile_lane < HEAD) if head == 0 else (tile_lane >= HEAD)
            mark = jnp.where(tile_lane == (1 - head) * HEAD, 1.0, 0.0).astype(jnp.bfloat16)
            scores = lax.dot_general(
                jnp.where(own, queries, mark), sides[head][0], (((1,), (1,)), ((), ())),
                preferred_element_type=jnp.float32,
            )
            top = jnp.max(scores, axis=-1, keepdims=True)
            probs = jnp.exp(scores - top).astype(jnp.bfloat16)
            mixed = jnp.dot(probs, sides[head][1], preferred_element_type=jnp.float32)
            parts.append(mixed / pltpu.roll(mixed, HEAD, 1))
        joined = jnp.where(tile_lane < HEAD, parts[0], parts[1])
        out_ref[0, at * tile : (at + 1) * tile, :] = joined.astype(out_ref.dtype)


def attention(projected, bias):
    images, rows, width = projected.shape
    pairs = width // 3 // PAIR
    tile = rows // 4 if rows % (4 * ROWS) == 0 else rows
    block = lambda first: pl.BlockSpec((1, rows, PAIR), lambda i, p: (i, 0, first + p))
    return pl.pallas_call(
        partial(attention_kernel, tile),
        grid=(images, pairs),
        in_specs=[block(0), block(pairs), block(2 * pairs), pl.BlockSpec((rows, PAIR), lambda i, p: (0, 0))],
        out_specs=pl.BlockSpec((1, rows, PAIR), lambda i, p: (i, 0, p)),
        out_shape=jax.ShapeDtypeStruct((images, rows, width // 3), jnp.bfloat16),
        compiler_params=pltpu.CompilerParams(vmem_limit_bytes=48 * 1024 * 1024),
        cost_estimate=pl.CostEstimate(
            flops=images * pairs * 2 * rows * rows * PAIR * 4,
            bytes_accessed=images * rows * width * 3,
            transcendentals=images * pairs * 2 * rows * rows,
        ),
        name="attention",
    )(projected, projected, projected, bias)


def by_image(tokens, parts, rows, slots):
    count = tokens.shape[0]
    each = parts // IMAGES
    out = jnp.arange(parts * slots, dtype=jnp.int32)
    part, at = out // slots, out % slots
    place = (part % each) * rows + at
    source = jnp.where((at < rows) & (place < count // IMAGES), place * IMAGES + part // each, -1)
    pick = (source[:, None] == jnp.arange(count, dtype=jnp.int32)[None, :]).astype(tokens.dtype)
    return jnp.dot(pick, tokens, preferred_element_type=jnp.float32).astype(tokens.dtype)


def plane_peers(m):
    core, x, y = m % 2, (m // 2) % 2, m // 4
    to_x, to_y = 2 - 4 * x, 4 - 8 * y
    return [m + to_x, m + to_y, m + to_x + to_y, m + 1 - 2 * core]


def remote(source, target, send_sem, recv_sem, member, part):
    return pltpu.make_async_remote_copy(
        src_ref=source, dst_ref=target, send_sem=send_sem, recv_sem=recv_sem,
        device_id={"member": member, "dp": part}, device_id_type=pl.DeviceIdType.MESH,
    )


def greet(m, z, dp):
    barrier = pltpu.get_barrier_semaphore()
    peers = plane_peers(m)
    for k in range(1, dp):
        pl.semaphore_signal(
            barrier, inc=1, device_id={"member": m, "dp": (z + k) % dp}, device_id_type=pl.DeviceIdType.MESH
        )
    for peer in peers:
        pl.semaphore_signal(
            barrier, inc=1, device_id={"member": peer, "dp": z}, device_id_type=pl.DeviceIdType.MESH
        )
    pl.semaphore_wait(barrier, dp - 1 + len(peers))


class PlaneGather:
    def __init__(self, source, out, m, z, sends, recvs):
        self.out, self.m, self.z, self.sends, self.recvs = out, m, z, sends, recvs
        self.peers = plane_peers(m)
        self.first = [
            remote(source, out.at[m], sends.at[p], recvs.at[p], self.peers[p], z) for p in range(4)
        ]
        self.second = []

    def start(self):
        for copy in self.first:
            copy.start()

    def forward(self):
        for p in range(3):
            here = self.out.at[self.peers[p]]
            self.first[p].wait_recv()
            copy = remote(here, here, self.sends.at[4 + p], self.recvs.at[4 + p], self.peers[3], self.z)
            copy.start()
            self.second.append(copy)

    def finish(self):
        self.first[3].wait_recv()
        for copy in self.second:
            copy.wait_recv()
        for copy in self.first + self.second:
            copy.wait_send()


def gather_kernel(
    dp, src, wts, head, tok, own, head_all,
    z_send, z_recv, p_send, p_recv, f_send, f_recv, w_send, w_recv, local, h_send, h_recv,
):
    rows, width = src.shape[1], src.shape[2]
    piece = wts.shape[1] // 3
    m, z = lax.axis_index("member"), lax.axis_index("dp")
    core = m % 2
    share = width // 4
    peers = plane_peers(m)
    other_core = peers[3]
    greet(m, z, dp)

    def columns(chip):
        return pl.ds(pl.multiple_of(chip * share, PAIR), share)

    def region(image, part, chip):
        return tok.at[image, pl.ds(pl.multiple_of(part * rows, ROWS), rows), columns(chip)]

    def send(source, target, sems, member, part):
        return pltpu.make_async_remote_copy(
            src_ref=source, dst_ref=target, send_sem=sems[0], recv_sem=sems[1],
            device_id={"member": member, "dp": part}, device_id_type=pl.DeviceIdType.MESH,
        )

    chip = m // 2
    first = []
    for k in range(1, dp):
        copy = send(
            src.at[core, :, columns(chip)], region(core, z, chip),
            (z_send.at[k - 1], z_recv.at[k - 1]), m, (z + k) % dp,
        )
        copy.start()
        first.append(copy)
    stay = pltpu.make_async_copy(src, tok.at[:, pl.ds(pl.multiple_of(z * rows, ROWS), rows), :], local.at[3])
    stay.start()
    head_stay = pltpu.make_async_copy(head, head_all.at[m], local.at[4])
    head_stay.start()
    heads = PlaneGather(head, head_all, m, z, h_send, h_recv)
    heads.start()

    def weight_copy(j):
        dest, slot = (3 * z + j) % dp, (3 * z + j) // dp
        source = wts.at[:, pl.ds(j * piece, piece)]
        target = own.at[:, pl.ds(pl.multiple_of(slot * piece, PAIR), piece)]
        return dest, source, target, slot

    passed = []
    for k in range(1, dp):
        part = (z + dp - k) % dp
        here = region(core, part, chip)
        first[k - 1].wait_recv()
        for p, peer in enumerate(peers):
            copy = send(here, here, (p_send.at[k - 1, p], p_recv.at[k - 1, p]), peer, z)
            copy.start()
            passed.append(copy)
    for copy in first:
        copy.wait_send()
    for j in range(3):
        dest, source, target, slot = weight_copy(j)

        @pl.when(dest == z)
        def _():
            pltpu.make_async_copy(source, target, local.at[j]).start()

        @pl.when(dest != z)
        def _():
            send(source, target, (w_send.at[j], w_recv.at[slot]), m, dest).start()

    heads.forward()
    chips_of = [peer // 2 for peer in peers[:3]]
    for k in range(1, dp):
        part = (z + dp - k) % dp
        for p in range(3):
            here = region(core, part, chips_of[p])
            send(here, here, (p_send.at[k - 1, p], p_recv.at[k - 1, p]), other_core, z).wait_recv()
            copy = send(here, here, (f_send.at[k - 1, p], f_recv.at[k - 1, p]), other_core, z)
            copy.start()
            passed.append(copy)
    for k in range(1, dp):
        part = (z + dp - k) % dp
        there = region(1 - core, part, chip)
        send(there, there, (p_send.at[k - 1, 3], p_recv.at[k - 1, 3]), other_core, z).wait_recv()
        for p in range(3):
            there = region(1 - core, part, chips_of[p])
            send(there, there, (f_send.at[k - 1, p], f_recv.at[k - 1, p]), other_core, z).wait_recv()
    heads.finish()
    head_stay.wait()
    for copy in passed:
        copy.wait_send()
    for j in range(3):
        dest, source, target, slot = weight_copy(j)

        @pl.when(dest == z)
        def _():
            pltpu.make_async_copy(source, target, local.at[j]).wait()

        @pl.when(dest != z)
        def _():
            send(source, target, (w_send.at[j], w_recv.at[slot]), m, dest).wait_send()

    for slot in range(3):
        place = own.at[:, pl.ds(slot * piece, piece)]

        @pl.when((slot * dp + z) // 3 != z)
        def _():
            send(place, place, (w_send.at[0], w_recv.at[slot]), m, (z + 1) % dp).wait_recv()

    stay.wait()


def gather_teacher(tokens, weights, head, dp, member):
    images, rows, width = tokens.shape
    steps = dp - 1
    dma = pltpu.SemaphoreType.DMA
    return pl.pallas_call(
        partial(gather_kernel, dp),
        out_shape=(
            jax.ShapeDtypeStruct((images, dp * rows, width), tokens.dtype),
            jax.ShapeDtypeStruct(weights.shape, weights.dtype),
            jax.ShapeDtypeStruct((member,) + head.shape, head.dtype),
        ),
        in_specs=[pl.BlockSpec(memory_space=pl.ANY)] * 3,
        out_specs=(pl.BlockSpec(memory_space=pl.ANY),) * 3,
        scratch_shapes=[
            dma((steps,)), dma((steps,)), dma((steps, 4)), dma((steps, 4)), dma((steps, 3)), dma((steps, 3)),
            dma((3,)), dma((3,)), dma((5,)), dma((7,)), dma((7,)),
        ],
        compiler_params=pltpu.CompilerParams(collective_id=0, has_side_effects=True),
        cost_estimate=pl.CostEstimate(
            flops=0, bytes_accessed=64 * images * dp * rows * width, transcendentals=0
        ),
        name="gather_teacher",
    )(tokens, weights, head)


def middle_kernel(
    dp, part_rows, own_rows, norm, context, own_out, head, grads, outs,
    pair, plane_out, plane_in, z_out, summed, pred, own_grad,
    c_send, c_recv, p_send, p_recv, z_send, z_recv, g_send, g_recv, o_send, o_recv,
):
    m, z = lax.axis_index("member"), lax.axis_index("dp")
    core, chip = m % 2, m // 2
    member, share, slots = context.shape[0], context.shape[2], own_out.shape[0]
    width = head.shape[0]
    peers = plane_peers(m)
    f32 = jnp.float32
    greet(m, z, dp)

    across = [
        remote(context.at[2 * c + 1 - core], pair.at[c], c_send.at[c], c_recv.at[c], peers[3], z)
        for c in range(member // 2)
    ]
    for copy in across:
        copy.start()
    out_gather = PlaneGather(own_out, outs, m, z, o_send, o_recv)
    for d in range(dp):
        at = slice(d * share, (d + 1) * share)
        pred[:, at] = lax.dot_general(
            own_out[...], head[at, :], (((1,), (1,)), ((), ())), preferred_element_type=f32
        )
    outs[pl.ds(m, 1)] = own_out[...][None]
    for copy in across:
        copy.wait_recv()
    in_plane = []
    for p in range(3):
        there = peers[p] // 2
        plane_out[p] = (context[peers[p]].astype(f32) + pair[there].astype(f32)).astype(jnp.bfloat16)
        copy = remote(plane_out.at[p], plane_in.at[p], p_send.at[p], p_recv.at[p], peers[p], z)
        copy.start()
        in_plane.append(copy)
    out_gather.start()
    total = context[m].astype(f32) + pair[chip].astype(f32)
    for p in range(3):
        in_plane[p].wait_recv()
        total = total + plane_in[p].astype(f32)
    fill = jnp.zeros((slots - own_rows, share), f32)
    for d in range(dp):
        block = jnp.concatenate([total[d * own_rows : (d + 1) * own_rows], fill], axis=0)
        z_out[d] = block.astype(jnp.bfloat16)
    over = []
    for k in range(1, dp):
        there = (z + k) % dp
        copy = remote(z_out.at[there], summed.at[z], z_send.at[k - 1], z_recv.at[k - 1], m, there)
        copy.start()
        over.append(copy)
    summed[pl.ds(z, 1)] = z_out[pl.ds(z, 1)]
    out_gather.forward()
    for copy in over:
        copy.wait_recv()
    blocks = [summed[d].astype(f32) for d in range(dp)]
    mean = sum(jnp.sum(b, axis=-1, keepdims=True) for b in blocks) / width
    square = sum(jnp.sum(b * b, axis=-1, keepdims=True) for b in blocks) / width
    scale = lax.rsqrt(square - mean * mean + 1e-06)
    quarter = part_rows_slots(part_rows) // own_rows
    row = lax.broadcasted_iota(jnp.int32, (slots, share), 0)
    place = (m % quarter) * own_rows + row
    real = (row < own_rows) & (place < part_rows) & (z * part_rows + place < VALID)
    for d in range(dp):
        at = slice(d * share, (d + 1) * share)
        target = (blocks[d] - mean) * scale
        own_grad[:, at] = jnp.where(real, (pred[:, at] - target) / norm, 0.0).astype(jnp.bfloat16)
    grad_gather = PlaneGather(own_grad, grads, m, z, g_send, g_recv)
    grad_gather.start()
    grads[pl.ds(m, 1)] = own_grad[...][None]
    grad_gather.forward()
    out_gather.finish()
    grad_gather.finish()
    for copy in across + in_plane + over:
        copy.wait_send()


def part_rows_slots(part_rows):
    return -(-part_rows // ROWS) * ROWS


def middle(context, own_out, head, dp, part_rows, own_rows):
    member, rows, share = context.shape
    slots, inner = own_out.shape
    width = head.shape[0]
    half = member // 2
    dma = pltpu.SemaphoreType.DMA
    vmem = lambda *shape: pltpu.VMEM(shape, jnp.bfloat16)
    whole = pl.BlockSpec(memory_space=pltpu.VMEM)
    return pl.pallas_call(
        partial(middle_kernel, dp, part_rows, own_rows, math.sqrt(IMAGES * VALID)),
        out_shape=(
            jax.ShapeDtypeStruct((member, slots, width), jnp.bfloat16),
            jax.ShapeDtypeStruct((member, slots, inner), jnp.bfloat16),
        ),
        in_specs=[whole] * 3,
        out_specs=(whole,) * 2,
        scratch_shapes=[
            vmem(half, rows, share), vmem(3, rows, share), vmem(3, rows, share),
            vmem(dp, slots, share), vmem(dp, slots, share),
            pltpu.VMEM((slots, width), jnp.float32), vmem(slots, width),
            dma((half,)), dma((half,)), dma((3,)), dma((3,)), dma((dp - 1,)), dma((dp - 1,)),
            dma((7,)), dma((7,)), dma((7,)), dma((7,)),
        ],
        compiler_params=pltpu.CompilerParams(
            collective_id=1, has_side_effects=True, vmem_limit_bytes=48 * 1024 * 1024
        ),
        cost_estimate=pl.CostEstimate(
            flops=2 * slots * width * inner, bytes_accessed=100 * 1024 * 1024, transcendentals=0
        ),
        name="context_to_pred_grad",
    )(context, own_out, head)


def split_body(dp, member, teacher_tokens, teacher_qkv, student_tokens, student_gain, w_up, w_down, w_head):
    part_rows = teacher_tokens.shape[0] // IMAGES
    slot_rows = part_rows_slots(part_rows)
    own_rows = IMAGES * slot_rows // member
    own_slots = part_rows_slots(own_rows)
    quarter = slot_rows // own_rows
    member_at = lax.axis_index("member")

    student = by_image(student_tokens, member, own_rows, own_slots)
    inputs = student.astype(jnp.float32)
    in_mean = jnp.mean(inputs, axis=-1, keepdims=True)
    in_var = jnp.mean((inputs - in_mean) ** 2, axis=-1, keepdims=True)
    normed = ((inputs - in_mean) * lax.rsqrt(in_var + 1e-06) * student_gain).astype(jnp.bfloat16)
    pre = jnp.dot(normed, w_up, preferred_element_type=jnp.float32)
    gelu_tanh = partial(jax.nn.gelu, approximate=True)
    hidden = gelu_tanh(pre).astype(jnp.bfloat16)
    branch_part = lax.dot_general(
        hidden, w_down, (((1,), (1,)), ((), ())), preferred_element_type=jnp.float32
    )
    teacher_slots, branch_part = lax.optimization_barrier((by_image(teacher_tokens, IMAGES, slot_rows, slot_rows), branch_part))
    teacher_slots = teacher_slots.reshape(IMAGES, slot_rows, -1)
    tokens, weights, head_all = gather_teacher(teacher_slots, teacher_qkv[0], w_head.T, dp, member)
    head_all = head_all.reshape(-1, w_head.shape[0])
    branch = lax.psum_scatter(branch_part, "member", scatter_dimension=0, tiled=True)
    own_inputs = lax.dynamic_slice_in_dim(student, member_at * own_slots, own_slots, 0).astype(jnp.float32)
    own_out = (own_inputs + branch).astype(jnp.bfloat16)

    images, rows, width = tokens.shape
    projected = jnp.dot(
        tokens.reshape(images * rows, width), weights, preferred_element_type=jnp.float32
    ).astype(jnp.bfloat16).reshape(images, rows, -1)
    key_row = jnp.arange(rows, dtype=jnp.int32)
    in_part = key_row % slot_rows
    real_key = (in_part < part_rows) & (key_row // slot_rows * part_rows + in_part < VALID)
    bias = jnp.broadcast_to(jnp.where(real_key, 0.0, -1e30).astype(jnp.bfloat16)[:, None], (rows, PAIR))
    context = attention(projected, bias)
    share = context.shape[-1]
    context = context.reshape(images, dp, quarter, own_rows, share).transpose(0, 2, 1, 3, 4)
    context = context.reshape(member, dp * own_rows, share)
    pred_grad, student_out = middle(context, own_out, head_all, dp, part_rows, own_rows)
    pred_grad = pred_grad.reshape(member * own_slots, width)
    student_out = student_out.reshape(member * own_slots, -1)

    head_width = w_head.shape[1]
    own_columns = lax.dynamic_slice_in_dim(pred_grad, member_at * head_width, head_width, 1)
    out_grad = lax.dot_general(
        pred_grad, head_all, (((1,), (0,)), ((), ())), preferred_element_type=jnp.float32
    ).astype(jnp.bfloat16)
    grad_down = lax.dot_general(
        out_grad, hidden, (((0,), (0,)), ((), ())), preferred_element_type=jnp.float32
    )
    hidden_grad = jnp.dot(out_grad, w_down, preferred_element_type=jnp.float32)
    _, pullback = jax.vjp(gelu_tanh, pre)
    pre_grad = pullback(hidden_grad)[0].astype(jnp.bfloat16)
    grad_up = lax.dot_general(
        normed, pre_grad, (((0,), (0,)), ((), ())), preferred_element_type=jnp.float32
    )
    grad_head = lax.dot_general(
        student_out, own_columns, (((0,), (0,)), ((), ())), preferred_element_type=jnp.float32
    )
    return tuple(
        lax.psum_scatter(g.astype(jnp.bfloat16), "dp", scatter_dimension=0, tiled=True).astype(jnp.float32)
        for g in (grad_up, grad_down, grad_head)
    )


def body(teacher_tokens, teacher_qkv, student_tokens, student_gain, w_up, w_down, w_head):
    tok_rows = teacher_tokens.shape[0]
    feat_width = teacher_tokens.shape[1]
    head_count = feat_width // 64
    own_columns = teacher_qkv[0]
    query_slots = lax.axis_index("dp") * tok_rows + jnp.arange(tok_rows, dtype=jnp.int32)
    query_image = query_slots % IMAGES
    real_query = query_slots // IMAGES < VALID
    projected = jnp.dot(
        teacher_tokens,
        lax.all_gather(own_columns, "dp", axis=1, tiled=True),
        preferred_element_type=jnp.float32,
    ).astype(jnp.bfloat16)
    queries = projected[:, :feat_width].reshape(tok_rows, head_count, 64)
    keys_local = projected[:, feat_width : 2 * feat_width]
    values_local = projected[:, 2 * feat_width :]
    row_max = jnp.full((head_count, tok_rows), -1e30, jnp.float32)
    weighted = jnp.zeros((tok_rows, head_count, 64), jnp.float32)
    key_heads = lax.all_gather(keys_local, "dp", axis=0, tiled=True).reshape(-1, head_count, 64)
    value_heads = lax.all_gather(values_local, "dp", axis=0, tiled=True).reshape(-1, head_count, 64)
    key_slots = jnp.arange(key_heads.shape[0], dtype=jnp.int32)
    allowed = (query_image[:, None] == (key_slots % IMAGES)[None, :]) & (
        key_slots // IMAGES < VALID
    )[None, :]
    scores = (
        jnp.einsum("qhd,khd->hqk", queries, key_heads, preferred_element_type=jnp.float32) * 0.125
    )
    scores = jnp.where(allowed[None], scores, -1e30)
    new_max = jnp.maximum(row_max, jnp.max(scores, axis=-1))
    factor = jnp.exp(row_max - new_max)
    expsc = jnp.where(allowed[None], jnp.exp(scores - new_max[:, :, None]), 0.0)
    denom_sum = jnp.sum(expsc, axis=-1)
    update = jnp.einsum(
        "hqk,khd->qhd", expsc.astype(jnp.bfloat16), value_heads, preferred_element_type=jnp.float32
    )
    weighted = weighted * factor.T[:, :, None] + update
    row_max, denom_sum, weighted = (new_max, denom_sum, weighted)
    context = (weighted / denom_sum.T[:, :, None]).reshape(tok_rows, feat_width)
    member_slot = lax.axis_index("member")
    share_width = feat_width // lax.axis_size("member")
    summed = lax.psum(context, "member")
    row_mean = jnp.mean(summed, axis=-1, keepdims=True)
    mean_square = jnp.mean(summed * summed, axis=-1, keepdims=True)
    full_target = (summed - row_mean) * lax.rsqrt(mean_square - row_mean * row_mean + 1e-06)
    target = lax.dynamic_slice_in_dim(full_target, member_slot * share_width, share_width, 1)
    inputs = student_tokens.astype(jnp.float32)
    in_mean = jnp.mean(inputs, axis=-1, keepdims=True)
    in_var = jnp.mean((inputs - in_mean) ** 2, axis=-1, keepdims=True)
    normed = ((inputs - in_mean) * lax.rsqrt(in_var + 1e-06) * student_gain).astype(jnp.bfloat16)
    pre = jnp.dot(normed, w_up, preferred_element_type=jnp.float32)
    gelu_tanh = partial(jax.nn.gelu, approximate=True)
    hidden = gelu_tanh(pre).astype(jnp.bfloat16)
    branch_part = lax.dot_general(
        hidden, w_down, (((1,), (1,)), ((), ())), preferred_element_type=jnp.float32
    )
    student_out = (inputs + lax.psum(branch_part, "member")).astype(jnp.bfloat16)
    pred = jnp.dot(student_out, w_head, preferred_element_type=jnp.float32)
    pred_grad = jnp.where(
        real_query[:, None], (pred - target) / math.sqrt(IMAGES * VALID), 0.0
    ).astype(jnp.bfloat16)
    grad_head = lax.dot_general(
        student_out, pred_grad, (((0,), (0,)), ((), ())), preferred_element_type=jnp.float32
    )
    out_part = lax.dot_general(
        pred_grad, w_head, (((1,), (1,)), ((), ())), preferred_element_type=jnp.float32
    )
    out_grad = lax.psum(out_part, "member").astype(jnp.bfloat16)
    grad_down = lax.dot_general(
        out_grad, hidden, (((0,), (0,)), ((), ())), preferred_element_type=jnp.float32
    )
    hidden_grad = jnp.dot(out_grad, w_down, preferred_element_type=jnp.float32)
    _, pullback = jax.vjp(gelu_tanh, pre)
    pre_grad = pullback(hidden_grad)[0].astype(jnp.bfloat16)
    grad_up = lax.dot_general(
        normed, pre_grad, (((0,), (0,)), ((), ())), preferred_element_type=jnp.float32
    )
    grad_up, grad_down, grad_head = (
        lax.psum_scatter(grad_up, "dp", scatter_dimension=0, tiled=True),
        lax.psum_scatter(grad_down, "dp", scatter_dimension=0, tiled=True),
        lax.psum_scatter(grad_head, "dp", scatter_dimension=0, tiled=True),
    )
    return (grad_up, grad_down, grad_head)


def can_split(dp, member, tokens, feat):
    slot_rows = -(-(tokens // dp // IMAGES) // ROWS) * ROWS
    return (
        math.gcd(3, dp) == 1
        and feat % (dp * PAIR) == 0
        and member == 4 * IMAGES
        and feat % (4 * PAIR) == 0
        and slot_rows * IMAGES % (member * 8) == 0
    )


def solution(mesh):
    in_specs = (
        P("dp", None),
        P("member", None, "dp"),
        P("dp", None),
        P(),
        P(None, "member"),
        P(None, "member"),
        P(None, "member"),
    )
    out_specs = (P("dp", "member"), P("dp", "member"), P("dp", "member"))

    def run(teacher_tokens, *rest):
        dp, member = mesh.shape["dp"], mesh.shape["member"]
        part = body
        if can_split(dp, member, *teacher_tokens.shape):
            part = partial(split_body, dp, member)
        call = jax.shard_map(part, mesh=mesh, in_specs=in_specs, out_specs=out_specs, check_vma=False)
        return call(teacher_tokens, *rest)

    return run
```

```python
from functools import partial
import math

import jax
import jax.numpy as jnp
from jax import lax
from jax.experimental import pallas as pl
from jax.experimental.pallas import tpu as pltpu
from jax.sharding import PartitionSpec as P

VALID = 1370
IMAGES = 2
HEAD = 64
PAIR = 2 * HEAD
ROWS = 16


def attention_kernel(tile, q_ref, k_ref, v_ref, bias_ref, out_ref):
    rows = q_ref.shape[1]
    lane = lax.broadcasted_iota(jnp.int32, (rows, PAIR), 1)
    keys, values = k_ref[0], v_ref[0]
    bias = bias_ref[...]
    sides = []
    for head in range(2):
        own = (lane < HEAD) if head == 0 else (lane >= HEAD)
        sides.append((jnp.where(own, keys, bias), jnp.where(own, values, jnp.ones_like(values))))
    tile_lane = lax.broadcasted_iota(jnp.int32, (tile, PAIR), 1)
    for at in range(rows // tile):
        queries = q_ref[0, at * tile : (at + 1) * tile, :] * jnp.asarray(0.125, jnp.bfloat16)
        parts = []
        for head in range(2):
            own = (tile_lane < HEAD) if head == 0 else (tile_lane >= HEAD)
            mark = jnp.where(tile_lane == (1 - head) * HEAD, 1.0, 0.0).astype(jnp.bfloat16)
            scores = lax.dot_general(
                jnp.where(own, queries, mark), sides[head][0], (((1,), (1,)), ((), ())),
                preferred_element_type=jnp.float32,
            )
            top = jnp.max(scores, axis=-1, keepdims=True)
            probs = jnp.exp(scores - top).astype(jnp.bfloat16)
            mixed = jnp.dot(probs, sides[head][1], preferred_element_type=jnp.float32)
            parts.append(mixed / pltpu.roll(mixed, HEAD, 1))
        joined = jnp.where(tile_lane < HEAD, parts[0], parts[1])
        out_ref[0, at * tile : (at + 1) * tile, :] = joined.astype(out_ref.dtype)


def attention(projected, bias):
    images, rows, width = projected.shape
    pairs = width // 3 // PAIR
    tile = rows // 4 if rows % (4 * ROWS) == 0 else rows
    block = lambda first: pl.BlockSpec((1, rows, PAIR), lambda i, p: (i, 0, first + p))
    return pl.pallas_call(
        partial(attention_kernel, tile),
        grid=(images, pairs),
        in_specs=[block(0), block(pairs), block(2 * pairs), pl.BlockSpec((rows, PAIR), lambda i, p: (0, 0))],
        out_specs=pl.BlockSpec((1, rows, PAIR), lambda i, p: (i, 0, p)),
        out_shape=jax.ShapeDtypeStruct((images, rows, width // 3), jnp.bfloat16),
        compiler_params=pltpu.CompilerParams(vmem_limit_bytes=48 * 1024 * 1024),
        cost_estimate=pl.CostEstimate(
            flops=images * pairs * 2 * rows * rows * PAIR * 4,
            bytes_accessed=images * rows * width * 3,
            transcendentals=images * pairs * 2 * rows * rows,
        ),
        name="attention",
    )(projected, projected, projected, bias)


def by_image(tokens, parts, rows, slots):
    count = tokens.shape[0]
    each = parts // IMAGES
    out = jnp.arange(parts * slots, dtype=jnp.int32)
    part, at = out // slots, out % slots
    place = (part % each) * rows + at
    source = jnp.where((at < rows) & (place < count // IMAGES), place * IMAGES + part // each, -1)
    pick = (source[:, None] == jnp.arange(count, dtype=jnp.int32)[None, :]).astype(tokens.dtype)
    return jnp.dot(pick, tokens, preferred_element_type=jnp.float32).astype(tokens.dtype)


def plane_peers(m):
    core, x, y = m % 2, (m // 2) % 2, m // 4
    to_x, to_y = 2 - 4 * x, 4 - 8 * y
    return [m + to_x, m + to_y, m + to_x + to_y, m + 1 - 2 * core]


def remote(source, target, send_sem, recv_sem, member, part):
    return pltpu.make_async_remote_copy(
        src_ref=source, dst_ref=target, send_sem=send_sem, recv_sem=recv_sem,
        device_id={"member": member, "dp": part}, device_id_type=pl.DeviceIdType.MESH,
    )


def greet(m, z, dp):
    barrier = pltpu.get_barrier_semaphore()
    peers = plane_peers(m)
    for k in range(1, dp):
        pl.semaphore_signal(
            barrier, inc=1, device_id={"member": m, "dp": (z + k) % dp}, device_id_type=pl.DeviceIdType.MESH
        )
    for peer in peers:
        pl.semaphore_signal(
            barrier, inc=1, device_id={"member": peer, "dp": z}, device_id_type=pl.DeviceIdType.MESH
        )
    pl.semaphore_wait(barrier, dp - 1 + len(peers))


class PlaneGather:
    def __init__(self, source, out, m, z, sends, recvs):
        self.out, self.m, self.z, self.sends, self.recvs = out, m, z, sends, recvs
        self.peers = plane_peers(m)
        self.first = [
            remote(source, out.at[m], sends.at[p], recvs.at[p], self.peers[p], z) for p in range(4)
        ]
        self.second = []

    def start(self):
        for copy in self.first:
            copy.start()

    def forward(self):
        for p in range(3):
            here = self.out.at[self.peers[p]]
            self.first[p].wait_recv()
            copy = remote(here, here, self.sends.at[4 + p], self.recvs.at[4 + p], self.peers[3], self.z)
            copy.start()
            self.second.append(copy)

    def finish(self):
        self.first[3].wait_recv()
        for copy in self.second:
            copy.wait_recv()
        for copy in self.first + self.second:
            copy.wait_send()


def gather_kernel(
    dp, src, wts, head, tok, own, head_all,
    z_send, z_recv, p_send, p_recv, f_send, f_recv, w_send, w_recv, local, h_send, h_recv,
):
    rows, width = src.shape[1], src.shape[2]
    piece = wts.shape[1] // 3
    m, z = lax.axis_index("member"), lax.axis_index("dp")
    core = m % 2
    share = width // 4
    peers = plane_peers(m)
    other_core = peers[3]
    greet(m, z, dp)

    def columns(chip):
        return pl.ds(pl.multiple_of(chip * share, PAIR), share)

    def region(image, part, chip):
        return tok.at[image, pl.ds(pl.multiple_of(part * rows, ROWS), rows), columns(chip)]

    def send(source, target, sems, member, part):
        return pltpu.make_async_remote_copy(
            src_ref=source, dst_ref=target, send_sem=sems[0], recv_sem=sems[1],
            device_id={"member": member, "dp": part}, device_id_type=pl.DeviceIdType.MESH,
        )

    chip = m // 2
    first = []
    for k in range(1, dp):
        copy = send(
            src.at[core, :, columns(chip)], region(core, z, chip),
            (z_send.at[k - 1], z_recv.at[k - 1]), m, (z + k) % dp,
        )
        copy.start()
        first.append(copy)
    stay = pltpu.make_async_copy(src, tok.at[:, pl.ds(pl.multiple_of(z * rows, ROWS), rows), :], local.at[3])
    stay.start()
    head_stay = pltpu.make_async_copy(head, head_all.at[m], local.at[4])
    head_stay.start()
    heads = PlaneGather(head, head_all, m, z, h_send, h_recv)
    heads.start()

    def weight_copy(j):
        dest, slot = (3 * z + j) % dp, (3 * z + j) // dp
        source = wts.at[:, pl.ds(j * piece, piece)]
        target = own.at[:, pl.ds(pl.multiple_of(slot * piece, PAIR), piece)]
        return dest, source, target, slot

    passed = []
    for k in range(1, dp):
        part = (z + dp - k) % dp
        here = region(core, part, chip)
        first[k - 1].wait_recv()
        for p, peer in enumerate(peers):
            copy = send(here, here, (p_send.at[k - 1, p], p_recv.at[k - 1, p]), peer, z)
            copy.start()
            passed.append(copy)
    for copy in first:
        copy.wait_send()
    for j in range(3):
        dest, source, target, slot = weight_copy(j)

        @pl.when(dest == z)
        def _():
            pltpu.make_async_copy(source, target, local.at[j]).start()

        @pl.when(dest != z)
        def _():
            send(source, target, (w_send.at[j], w_recv.at[slot]), m, dest).start()

    heads.forward()
    chips_of = [peer // 2 for peer in peers[:3]]
    for k in range(1, dp):
        part = (z + dp - k) % dp
        for p in range(3):
            here = region(core, part, chips_of[p])
            send(here, here, (p_send.at[k - 1, p], p_recv.at[k - 1, p]), other_core, z).wait_recv()
            copy = send(here, here, (f_send.at[k - 1, p], f_recv.at[k - 1, p]), other_core, z)
            copy.start()
            passed.append(copy)
    for k in range(1, dp):
        part = (z + dp - k) % dp
        there = region(1 - core, part, chip)
        send(there, there, (p_send.at[k - 1, 3], p_recv.at[k - 1, 3]), other_core, z).wait_recv()
        for p in range(3):
            there = region(1 - core, part, chips_of[p])
            send(there, there, (f_send.at[k - 1, p], f_recv.at[k - 1, p]), other_core, z).wait_recv()
    heads.finish()
    head_stay.wait()
    for copy in passed:
        copy.wait_send()
    for j in range(3):
        dest, source, target, slot = weight_copy(j)

        @pl.when(dest == z)
        def _():
            pltpu.make_async_copy(source, target, local.at[j]).wait()

        @pl.when(dest != z)
        def _():
            send(source, target, (w_send.at[j], w_recv.at[slot]), m, dest).wait_send()

    for slot in range(3):
        place = own.at[:, pl.ds(slot * piece, piece)]

        @pl.when((slot * dp + z) // 3 != z)
        def _():
            send(place, place, (w_send.at[0], w_recv.at[slot]), m, (z + 1) % dp).wait_recv()

    stay.wait()


def gather_teacher(tokens, weights, head, dp, member):
    images, rows, width = tokens.shape
    steps = dp - 1
    dma = pltpu.SemaphoreType.DMA
    return pl.pallas_call(
        partial(gather_kernel, dp),
        out_shape=(
            jax.ShapeDtypeStruct((images, dp * rows, width), tokens.dtype),
            jax.ShapeDtypeStruct(weights.shape, weights.dtype),
            jax.ShapeDtypeStruct((member,) + head.shape, head.dtype),
        ),
        in_specs=[pl.BlockSpec(memory_space=pl.ANY)] * 3,
        out_specs=(pl.BlockSpec(memory_space=pl.ANY),) * 3,
        scratch_shapes=[
            dma((steps,)), dma((steps,)), dma((steps, 4)), dma((steps, 4)), dma((steps, 3)), dma((steps, 3)),
            dma((3,)), dma((3,)), dma((5,)), dma((7,)), dma((7,)),
        ],
        compiler_params=pltpu.CompilerParams(collective_id=0, has_side_effects=True),
        cost_estimate=pl.CostEstimate(
            flops=0, bytes_accessed=64 * images * dp * rows * width, transcendentals=0
        ),
        name="gather_teacher",
    )(tokens, weights, head)


def middle_kernel(
    dp, part_rows, own_rows, norm, context, own_out, head, grads, outs,
    pair, plane_out, plane_in, z_out, summed, pred, own_grad,
    c_send, c_recv, p_send, p_recv, z_send, z_recv, g_send, g_recv, o_send, o_recv,
):
    m, z = lax.axis_index("member"), lax.axis_index("dp")
    core, chip = m % 2, m // 2
    member, share, slots = context.shape[0], context.shape[2], own_out.shape[0]
    width = head.shape[0]
    peers = plane_peers(m)
    f32 = jnp.float32
    greet(m, z, dp)

    across = [
        remote(context.at[2 * c + 1 - core], pair.at[c], c_send.at[c], c_recv.at[c], peers[3], z)
        for c in range(member // 2)
    ]
    for copy in across:
        copy.start()
    out_gather = PlaneGather(own_out, outs, m, z, o_send, o_recv)
    for d in range(dp):
        at = slice(d * share, (d + 1) * share)
        pred[:, at] = lax.dot_general(
            own_out[...], head[at, :], (((1,), (1,)), ((), ())), preferred_element_type=f32
        )
    outs[pl.ds(m, 1)] = own_out[...][None]
    for copy in across:
        copy.wait_recv()
    in_plane = []
    for p in range(3):
        there = peers[p] // 2
        plane_out[p] = (context[peers[p]].astype(f32) + pair[there].astype(f32)).astype(jnp.bfloat16)
        copy = remote(plane_out.at[p], plane_in.at[p], p_send.at[p], p_recv.at[p], peers[p], z)
        copy.start()
        in_plane.append(copy)
    out_gather.start()
    total = context[m].astype(f32) + pair[chip].astype(f32)
    for p in range(3):
        in_plane[p].wait_recv()
        total = total + plane_in[p].astype(f32)
    fill = jnp.zeros((slots - own_rows, share), f32)
    for d in range(dp):
        block = jnp.concatenate([total[d * own_rows : (d + 1) * own_rows], fill], axis=0)
        z_out[d] = block.astype(jnp.bfloat16)
    over = []
    for k in range(1, dp):
        there = (z + k) % dp
        copy = remote(z_out.at[there], summed.at[z], z_send.at[k - 1], z_recv.at[k - 1], m, there)
        copy.start()
        over.append(copy)
    summed[pl.ds(z, 1)] = z_out[pl.ds(z, 1)]
    out_gather.forward()
    for copy in over:
        copy.wait_recv()
    blocks = [summed[d].astype(f32) for d in range(dp)]
    mean = sum(jnp.sum(b, axis=-1, keepdims=True) for b in blocks) / width
    square = sum(jnp.sum(b * b, axis=-1, keepdims=True) for b in blocks) / width
    scale = lax.rsqrt(square - mean * mean + 1e-06)
    quarter = part_rows_slots(part_rows) // own_rows
    row = lax.broadcasted_iota(jnp.int32, (slots, share), 0)
    place = (m % quarter) * own_rows + row
    real = (row < own_rows) & (place < part_rows) & (z * part_rows + place < VALID)
    for d in range(dp):
        at = slice(d * share, (d + 1) * share)
        target = (blocks[d] - mean) * scale
        own_grad[:, at] = jnp.where(real, (pred[:, at] - target) / norm, 0.0).astype(jnp.bfloat16)
    grad_gather = PlaneGather(own_grad, grads, m, z, g_send, g_recv)
    grad_gather.start()
    grads[pl.ds(m, 1)] = own_grad[...][None]
    grad_gather.forward()
    out_gather.finish()
    grad_gather.finish()
    for copy in across + in_plane + over:
        copy.wait_send()


def part_rows_slots(part_rows):
    return -(-part_rows // ROWS) * ROWS


def middle(context, own_out, head, dp, part_rows, own_rows):
    member, rows, share = context.shape
    slots, inner = own_out.shape
    width = head.shape[0]
    half = member // 2
    dma = pltpu.SemaphoreType.DMA
    vmem = lambda *shape: pltpu.VMEM(shape, jnp.bfloat16)
    whole = pl.BlockSpec(memory_space=pltpu.VMEM)
    return pl.pallas_call(
        partial(middle_kernel, dp, part_rows, own_rows, math.sqrt(IMAGES * VALID)),
        out_shape=(
            jax.ShapeDtypeStruct((member, slots, width), jnp.bfloat16),
            jax.ShapeDtypeStruct((member, slots, inner), jnp.bfloat16),
        ),
        in_specs=[whole] * 3,
        out_specs=(whole,) * 2,
        scratch_shapes=[
            vmem(half, rows, share), vmem(3, rows, share), vmem(3, rows, share),
            vmem(dp, slots, share), vmem(dp, slots, share),
            pltpu.VMEM((slots, width), jnp.float32), vmem(slots, width),
            dma((half,)), dma((half,)), dma((3,)), dma((3,)), dma((dp - 1,)), dma((dp - 1,)),
            dma((7,)), dma((7,)), dma((7,)), dma((7,)),
        ],
        compiler_params=pltpu.CompilerParams(
            collective_id=1, has_side_effects=True, vmem_limit_bytes=48 * 1024 * 1024
        ),
        cost_estimate=pl.CostEstimate(
            flops=2 * slots * width * inner, bytes_accessed=100 * 1024 * 1024, transcendentals=0
        ),
        name="context_to_pred_grad",
    )(context, own_out, head)


def split_body(dp, member, teacher_tokens, teacher_qkv, student_tokens, student_gain, w_up, w_down, w_head):
    part_rows = teacher_tokens.shape[0] // IMAGES
    slot_rows = part_rows_slots(part_rows)
    own_rows = IMAGES * slot_rows // member
    own_slots = part_rows_slots(own_rows)
    quarter = slot_rows // own_rows
    member_at = lax.axis_index("member")

    student = by_image(student_tokens, member, own_rows, own_slots)
    inputs = student.astype(jnp.float32)
    in_mean = jnp.mean(inputs, axis=-1, keepdims=True)
    in_var = jnp.mean((inputs - in_mean) ** 2, axis=-1, keepdims=True)
    normed = ((inputs - in_mean) * lax.rsqrt(in_var + 1e-06) * student_gain).astype(jnp.bfloat16)
    pre = jnp.dot(normed, w_up, preferred_element_type=jnp.float32)
    gelu_tanh = partial(jax.nn.gelu, approximate=True)
    hidden = gelu_tanh(pre).astype(jnp.bfloat16)
    branch_part = lax.dot_general(
        hidden, w_down, (((1,), (1,)), ((), ())), preferred_element_type=jnp.float32
    )
    teacher_slots, branch_part = lax.optimization_barrier((by_image(teacher_tokens, IMAGES, slot_rows, slot_rows), branch_part))
    teacher_slots = teacher_slots.reshape(IMAGES, slot_rows, -1)
    tokens, weights, head_all = gather_teacher(teacher_slots, teacher_qkv[0], w_head.T, dp, member)
    head_all = head_all.reshape(-1, w_head.shape[0])
    tokens, branch_part = lax.optimization_barrier((tokens, branch_part))
    branch = lax.psum_scatter(branch_part, "member", scatter_dimension=0, tiled=True)
    own_inputs = lax.dynamic_slice_in_dim(student, member_at * own_slots, own_slots, 0).astype(jnp.float32)
    own_out = (own_inputs + branch).astype(jnp.bfloat16)

    images, rows, width = tokens.shape
    projected = jnp.dot(
        tokens.reshape(images * rows, width), weights, preferred_element_type=jnp.float32
    ).astype(jnp.bfloat16).reshape(images, rows, -1)
    key_row = jnp.arange(rows, dtype=jnp.int32)
    in_part = key_row % slot_rows
    real_key = (in_part < part_rows) & (key_row // slot_rows * part_rows + in_part < VALID)
    bias = jnp.broadcast_to(jnp.where(real_key, 0.0, -1e30).astype(jnp.bfloat16)[:, None], (rows, PAIR))
    context = attention(projected, bias)
    share = context.shape[-1]
    context = context.reshape(images, dp, quarter, own_rows, share).transpose(0, 2, 1, 3, 4)
    context = context.reshape(member, dp * own_rows, share)
    pred_grad, student_out = middle(context, own_out, head_all, dp, part_rows, own_rows)
    pred_grad = pred_grad.reshape(member * own_slots, width)
    student_out = student_out.reshape(member * own_slots, -1)

    def scatter(grad):
        return lax.psum_scatter(grad, "dp", scatter_dimension=0, tiled=True).astype(jnp.float32)

    def tokens_product(left, right):
        product = lax.dot_general(left, right, (((0,), (0,)), ((), ())), preferred_element_type=jnp.float32)
        return product.astype(jnp.bfloat16)

    head_width = w_head.shape[1]
    own_columns = lax.dynamic_slice_in_dim(pred_grad, member_at * head_width, head_width, 1)
    grad_head = tokens_product(student_out, own_columns)
    pred_grad, grad_head = lax.optimization_barrier((pred_grad, grad_head))
    grad_head = scatter(grad_head)
    out_grad = lax.dot_general(
        pred_grad, head_all, (((1,), (0,)), ((), ())), preferred_element_type=jnp.float32
    ).astype(jnp.bfloat16)
    grad_down = tokens_product(out_grad, hidden)
    out_grad, grad_down = lax.optimization_barrier((out_grad, grad_down))
    out_grad, grad_head = lax.optimization_barrier((out_grad, grad_head))
    grad_down = scatter(grad_down)
    hidden_grad = jnp.dot(out_grad, w_down, preferred_element_type=jnp.float32)
    _, pullback = jax.vjp(gelu_tanh, pre)
    pre_grad = pullback(hidden_grad)[0].astype(jnp.bfloat16)
    grad_up = scatter(tokens_product(normed, pre_grad))
    return grad_up, grad_down, grad_head


def body(teacher_tokens, teacher_qkv, student_tokens, student_gain, w_up, w_down, w_head):
    tok_rows = teacher_tokens.shape[0]
    feat_width = teacher_tokens.shape[1]
    head_count = feat_width // 64
    own_columns = teacher_qkv[0]
    query_slots = lax.axis_index("dp") * tok_rows + jnp.arange(tok_rows, dtype=jnp.int32)
    query_image = query_slots % IMAGES
    real_query = query_slots // IMAGES < VALID
    projected = jnp.dot(
        teacher_tokens,
        lax.all_gather(own_columns, "dp", axis=1, tiled=True),
        preferred_element_type=jnp.float32,
    ).astype(jnp.bfloat16)
    queries = projected[:, :feat_width].reshape(tok_rows, head_count, 64)
    keys_local = projected[:, feat_width : 2 * feat_width]
    values_local = projected[:, 2 * feat_width :]
    row_max = jnp.full((head_count, tok_rows), -1e30, jnp.float32)
    weighted = jnp.zeros((tok_rows, head_count, 64), jnp.float32)
    key_heads = lax.all_gather(keys_local, "dp", axis=0, tiled=True).reshape(-1, head_count, 64)
    value_heads = lax.all_gather(values_local, "dp", axis=0, tiled=True).reshape(-1, head_count, 64)
    key_slots = jnp.arange(key_heads.shape[0], dtype=jnp.int32)
    allowed = (query_image[:, None] == (key_slots % IMAGES)[None, :]) & (
        key_slots // IMAGES < VALID
    )[None, :]
    scores = (
        jnp.einsum("qhd,khd->hqk", queries, key_heads, preferred_element_type=jnp.float32) * 0.125
    )
    scores = jnp.where(allowed[None], scores, -1e30)
    new_max = jnp.maximum(row_max, jnp.max(scores, axis=-1))
    factor = jnp.exp(row_max - new_max)
    expsc = jnp.where(allowed[None], jnp.exp(scores - new_max[:, :, None]), 0.0)
    denom_sum = jnp.sum(expsc, axis=-1)
    update = jnp.einsum(
        "hqk,khd->qhd", expsc.astype(jnp.bfloat16), value_heads, preferred_element_type=jnp.float32
    )
    weighted = weighted * factor.T[:, :, None] + update
    row_max, denom_sum, weighted = (new_max, denom_sum, weighted)
    context = (weighted / denom_sum.T[:, :, None]).reshape(tok_rows, feat_width)
    member_slot = lax.axis_index("member")
    share_width = feat_width // lax.axis_size("member")
    summed = lax.psum(context, "member")
    row_mean = jnp.mean(summed, axis=-1, keepdims=True)
    mean_square = jnp.mean(summed * summed, axis=-1, keepdims=True)
    full_target = (summed - row_mean) * lax.rsqrt(mean_square - row_mean * row_mean + 1e-06)
    target = lax.dynamic_slice_in_dim(full_target, member_slot * share_width, share_width, 1)
    inputs = student_tokens.astype(jnp.float32)
    in_mean = jnp.mean(inputs, axis=-1, keepdims=True)
    in_var = jnp.mean((inputs - in_mean) ** 2, axis=-1, keepdims=True)
    normed = ((inputs - in_mean) * lax.rsqrt(in_var + 1e-06) * student_gain).astype(jnp.bfloat16)
    pre = jnp.dot(normed, w_up, preferred_element_type=jnp.float32)
    gelu_tanh = partial(jax.nn.gelu, approximate=True)
    hidden = gelu_tanh(pre).astype(jnp.bfloat16)
    branch_part = lax.dot_general(
        hidden, w_down, (((1,), (1,)), ((), ())), preferred_element_type=jnp.float32
    )
    student_out = (inputs + lax.psum(branch_part, "member")).astype(jnp.bfloat16)
    pred = jnp.dot(student_out, w_head, preferred_element_type=jnp.float32)
    pred_grad = jnp.where(
        real_query[:, None], (pred - target) / math.sqrt(IMAGES * VALID), 0.0
    ).astype(jnp.bfloat16)
    grad_head = lax.dot_general(
        student_out, pred_grad, (((0,), (0,)), ((), ())), preferred_element_type=jnp.float32
    )
    out_part = lax.dot_general(
        pred_grad, w_head, (((1,), (1,)), ((), ())), preferred_element_type=jnp.float32
    )
    out_grad = lax.psum(out_part, "member").astype(jnp.bfloat16)
    grad_down = lax.dot_general(
        out_grad, hidden, (((0,), (0,)), ((), ())), preferred_element_type=jnp.float32
    )
    hidden_grad = jnp.dot(out_grad, w_down, preferred_element_type=jnp.float32)
    _, pullback = jax.vjp(gelu_tanh, pre)
    pre_grad = pullback(hidden_grad)[0].astype(jnp.bfloat16)
    grad_up = lax.dot_general(
        normed, pre_grad, (((0,), (0,)), ((), ())), preferred_element_type=jnp.float32
    )
    grad_up, grad_down, grad_head = (
        lax.psum_scatter(grad_up, "dp", scatter_dimension=0, tiled=True),
        lax.psum_scatter(grad_down, "dp", scatter_dimension=0, tiled=True),
        lax.psum_scatter(grad_head, "dp", scatter_dimension=0, tiled=True),
    )
    return (grad_up, grad_down, grad_head)


def can_split(dp, member, tokens, feat):
    slot_rows = -(-(tokens // dp // IMAGES) // ROWS) * ROWS
    return (
        math.gcd(3, dp) == 1
        and feat % (dp * PAIR) == 0
        and member == 4 * IMAGES
        and feat % (4 * PAIR) == 0
        and slot_rows * IMAGES % (member * 8) == 0
    )


def solution(mesh):
    in_specs = (
        P("dp", None),
        P("member", None, "dp"),
        P("dp", None),
        P(),
        P(None, "member"),
        P(None, "member"),
        P(None, "member"),
    )
    out_specs = (P("dp", "member"), P("dp", "member"), P("dp", "member"))

    def run(teacher_tokens, *rest):
        dp, member = mesh.shape["dp"], mesh.shape["member"]
        part = body
        if can_split(dp, member, *teacher_tokens.shape):
            part = partial(split_body, dp, member)
        call = jax.shard_map(part, mesh=mesh, in_specs=in_specs, out_specs=out_specs, check_vma=False)
        return call(teacher_tokens, *rest)

    return run
```
